32 devices in a mesh: replica: 2 (over x), owner: 4 (over z), tensor: 4 (over y, core).
Axes of the slice: x: 2, y: 2, z: 4, core: 2. Of those that a mesh axis runs over, the one named last changes fastest.
Arguments:
- context: bfloat16 [4096, 8192], P(('replica', 'owner'), 'tensor'), parts along dimension 0, may hold values from -6 to 6
- output_weight: bfloat16 [8192, 8192], P('tensor'), may hold values from -0.09375 to 0.09375
- adapter_down: bfloat16 [64, 8192, 64], P('owner', 'tensor'), may hold values from -0.0625 to 0.0625
- adapter_up: bfloat16 [64, 64, 8192], P('owner', None, 'tensor'), may hold values from -0.75 to 0.75
- token_adapter: int32 [4096], P(('replica', 'owner')), parts along dimension 0, may hold values from 0 to 63, as said below
Outputs:
- projected: bfloat16 [4096, 8192], P(('replica', 'owner'), 'tensor'), parts along dimension 0
The draws below stay inside these ranges and needn't reach their ends.
There are 2 independent parts, one for each index of `replica`. The reference program is written for one: setup_inputs(seed, part) draws one part's arguments, and reference() takes and returns one part's arrays. A program takes and returns all parts, laid end to end along the dimension named above; an argument that names none is the same for every part. Nothing has to cross between parts.
Inputs may be any that keep to these rules, and one draw needn't show every extreme that they name: `token_adapter`: adapter a belongs to owner a // 16. In each owner index's block of 512 consecutive tokens at most 256 tokens name adapters of one owner; one owner, the same for all blocks of a draw, is named by exactly 256 tokens of every block.
All inputs are finite; a program needn't handle non-finite values.
Results may differ from the reference program's by a relative error of at most 0.013.
Values may be sent and summed in bfloat16 or wider, within the bound.
A program may use at most 256 MiB of HBM per device.

```python
import jax
import jax.numpy as jnp
from jax import lax

MODEL_WIDTH = 8192
ADAPTER_RANK = 64
TOK_OWN = 512
ADP_OWN = 16
CAP = 256
TOKENS = 2048
ADAPTER_COUNT = 64
N_OWNER = 4
N_TENSOR = 4


def draw_token_adapter(key, part):
    key = jax.random.fold_in(key, 11)
    key_hot, key_perm, key_local, key_other = jax.random.split(key, 4)
    hot_owner = jax.random.randint(key_hot, (), 0, N_OWNER)
    orders = jax.vmap(lambda single: jax.random.permutation(single, TOK_OWN))(jax.random.split(key_perm, N_OWNER))
    is_hot = orders < CAP
    local_ids = jax.random.randint(key_local, (N_OWNER, TOK_OWN), 0, ADP_OWN)
    others = jax.random.randint(key_other, (N_OWNER, TOK_OWN), 0, N_OWNER - 1)
    others = others + (others >= hot_owner).astype(jnp.int32)
    owner_of = jnp.where(is_hot, hot_owner, others)
    return (owner_of * ADP_OWN + local_ids).reshape(-1).astype(jnp.int32)


def with_spikes(values, own_key, source, target, blocks, factor):
    def block_of(dim):
        return (jnp.arange(values.shape[dim]) // (values.shape[dim] // blocks)).reshape((-1,) + (1,) * (values.ndim - 1 - dim))

    near = jax.random.permutation(own_key, blocks)[block_of(target)]
    other_side = (block_of(target) + blocks // 2) % blocks
    return jnp.where((block_of(source) == near) | (block_of(source) == other_side), factor * values, values)


def level_of(key, extent, cuts, smallest, top_value):
    factor_of, own = 1.0, jax.random.fold_in(key, 6)
    for position, parts in cuts:
        steps = jnp.exp(jax.random.uniform(jax.random.fold_in(own, position), (parts,), jnp.float32, smallest / len(cuts), top_value / len(cuts)))
        factor_of = factor_of * jnp.repeat(steps, extent[position] // parts).reshape([-1 if axis == position else 1 for axis in range(len(extent))])
    return factor_of


def bell_draw(stream_key, shape, spread, bound, cuts=(), held_as=jnp.bfloat16):
    result = spread * jax.random.normal(stream_key, shape, jnp.float32)
    if cuts:
        result = result * level_of(stream_key, shape, cuts, -0.22, 0.18)
    return jnp.clip(result, -bound, bound).astype(held_as)


def gaussian_with(rng, shape, spread, most, cuts, heavy, dtype=jnp.bfloat16):
    result = spread * jax.random.normal(rng, shape, jnp.float32)
    if cuts:
        result = result * level_of(rng, shape, cuts, -0.22, 0.18)
    return jnp.clip(with_spikes(result, jax.random.fold_in(rng, 3), *heavy), -most, most).astype(dtype)


def setup_inputs(seed: int = 0, part: int = 0) -> dict:
    key_of = jax.random.split(jax.random.key(seed), 6)
    part_keys = jax.random.split(jax.random.fold_in(key_of[5], part), 6)
    return {
        "context": bell_draw(part_keys[0], (TOKENS, MODEL_WIDTH), 1.0, 6.0, ((0, 4), (1, 4))),
        "output_weight": gaussian_with(key_of[1], (MODEL_WIDTH, MODEL_WIDTH), MODEL_WIDTH ** -0.5, 0.09375, ((0, 4),), (0, 1, 4, 2.0)),
        "adapter_down": bell_draw(key_of[2], (ADAPTER_COUNT, MODEL_WIDTH, ADAPTER_RANK), MODEL_WIDTH ** -0.5, 0.0625, ((0, 4), (1, 4))),
        "adapter_up": bell_draw(key_of[3], (ADAPTER_COUNT, ADAPTER_RANK, MODEL_WIDTH), ADAPTER_RANK ** -0.5, 0.75, ((0, 4), (2, 4))),
        "token_adapter": draw_token_adapter(jax.random.fold_in(jax.random.fold_in(key_of[5], part), 71), part),
    }


def reference(context, output_weight, adapter_down, adapter_up, token_adapter):
    row_count = context.shape[0]
    feature_block = MODEL_WIDTH // N_TENSOR
    output_sum = jnp.zeros((row_count, MODEL_WIDTH), jnp.float32)
    for block_index in range(N_TENSOR):
        lower_edge = block_index * feature_block
        partial_term = jnp.dot(context[:, lower_edge:lower_edge + feature_block], output_weight[lower_edge:lower_edge + feature_block, :], preferred_element_type=jnp.float32)
        rounded = lax.optimization_barrier(partial_term.astype(jnp.bfloat16))
        output_sum = output_sum + rounded.astype(jnp.float32)
    block_rows = 128 if row_count % 128 == 0 else row_count

    def adapter_block(input_rows):
        rows_in, incoming_index = input_rows
        down_matrices = adapter_down[incoming_index].astype(jnp.float32)
        reduced = jnp.einsum('td,tdr->tr', rows_in.astype(jnp.float32), down_matrices).astype(jnp.bfloat16)
        up_matrices = adapter_up[incoming_index].astype(jnp.float32)
        return jnp.einsum('tr,trd->td', reduced.astype(jnp.float32), up_matrices).astype(jnp.bfloat16)

    adapter_terms = lax.map(adapter_block, (context.reshape(-1, block_rows, MODEL_WIDTH), token_adapter.reshape(-1, block_rows))).reshape(row_count, MODEL_WIDTH)
    return (output_sum + adapter_terms.astype(jnp.float32)).astype(jnp.bfloat16)
```

```python
import jax
import jax.numpy as jnp
from jax import lax
from jax.sharding import PartitionSpec as P

BF16 = jnp.bfloat16
F32 = jnp.float32


def rank_in_owner(ids, per_adapter, owners):
    tokens = ids.shape[1]
    target = ids // per_adapter
    onehot = (target[:, :, None] == jnp.arange(owners)[None, None, :]).astype(BF16)
    before = (jnp.arange(tokens)[:, None] > jnp.arange(tokens)[None, :]).astype(BF16)
    counts = jnp.einsum("tu,buo->bto", before, onehot, preferred_element_type=F32)
    rank = jnp.sum(counts * onehot.astype(F32), axis=2).astype(jnp.int32)
    return target, rank


def on_device(context, output_weight, adapter_down, adapter_up, token_adapter):
    owners = lax.axis_size("owner")
    me = lax.axis_index("owner")
    tokens, features = context.shape
    per_adapter, _, rank_extent = adapter_down.shape
    capacity = tokens // 2
    chunks = 2
    slots = capacity // chunks
    wide = per_adapter * rank_extent

    all_ids = lax.all_gather(token_adapter, "owner", axis=0, tiled=False)
    target, rank = rank_in_owner(token_adapter[None], per_adapter, owners)
    target, rank = target[0], rank[0]

    places, sent = [], []
    for chunk in range(chunks):
        slot = jnp.where(rank // slots == chunk, target * slots + rank % slots, -1)
        place = (slot[:, None] == jnp.arange(owners * slots)[None, :]).astype(BF16)
        outgoing = lax.dot_general(
            place, context, (((0,), (0,)), ((), ())), preferred_element_type=F32
        ).astype(BF16)
        arrived = lax.all_to_all(
            outgoing.reshape(owners, slots, features), "owner", 0, 0, tiled=True
        ).reshape(owners * slots, features)
        places.append(place)
        sent.append(arrived)

    partial_out = jnp.dot(context, output_weight, preferred_element_type=F32).astype(BF16)
    output_sum = lax.psum_scatter(partial_out, "tensor", scatter_dimension=1, tiled=True)

    down = adapter_down.transpose(1, 0, 2).reshape(features, wide)
    up = adapter_up.reshape(wide, features)
    pick = (
        jnp.arange(wide)[:, None] % rank_extent == jnp.arange(rank_extent)[None, :]
    ).astype(BF16)
    block_of = jnp.arange(wide)[None, :] // rank_extent

    all_target, all_rank = rank_in_owner(all_ids, per_adapter, owners)
    all_within = jnp.where(all_target == me, all_ids % per_adapter, -1)

    back = []
    for chunk in range(chunks):
        here = all_rank[:, :, None] == (chunk * slots + jnp.arange(slots))[None, None, :]
        ids = jnp.max(jnp.where(here, all_within[:, :, None], -1), axis=1).reshape(-1)
        mask = ids[:, None] == block_of
        full = jnp.dot(sent[chunk], down, preferred_element_type=F32)
        full = jnp.where(mask, full, 0.0).astype(BF16)
        partial_rank = jnp.dot(full, pick, preferred_element_type=F32).astype(BF16)
        reduced = lax.psum(partial_rank, "tensor")
        spread = lax.dot_general(
            reduced, pick, (((1,), (1,)), ((), ())), preferred_element_type=F32
        )
        spread = jnp.where(mask, spread, 0.0).astype(BF16)
        lifted = jnp.dot(spread, up, preferred_element_type=F32).astype(BF16)
        back.append(
            lax.all_to_all(
                lifted.reshape(owners, slots, features), "owner", 0, 0, tiled=True
            ).reshape(owners * slots, features)
        )

    total = output_sum.astype(F32)
    for chunk in range(chunks):
        total = total + jnp.dot(places[chunk], back[chunk], preferred_element_type=F32)
    return total.astype(BF16)


def solution(mesh):
    placed = (
        P(("replica", "owner"), "tensor"),
        P("tensor", None),
        P("owner", "tensor", None),
        P("owner", None, "tensor"),
        P(("replica", "owner")),
    )
    return jax.shard_map(
        on_device,
        mesh=mesh,
        in_specs=placed,
        out_specs=P(("replica", "owner"), "tensor"),
        check_vma=False,
    )
```

```python
import functools

import jax
import jax.numpy as jnp
from jax import lax
from jax.experimental import pallas as pl
from jax.experimental.pallas import tpu as pltpu
from jax.sharding import PartitionSpec as P

BF16 = jnp.bfloat16
F32 = jnp.float32
MESH = pl.DeviceIdType.MESH
CORES = 2
CHUNKS = 2


def remote(src, dst, send, recv, axis, index):
    return pltpu.make_async_remote_copy(
        src_ref=src,
        dst_ref=dst,
        send_sem=send,
        recv_sem=recv,
        device_id={axis: index},
        device_id_type=MESH,
    )


def kernel(
    owners,
    tensors,
    tile,
    ctx_ref,
    w_ref,
    down_ref,
    up_ref,
    outgoing_ref,
    ids_out_ref,
    place_ref,
    out_ref,
    arrived,
    ids_in,
    stage,
    down,
    up,
    wbuf,
    pair_out,
    pair_in,
    far_out,
    far_in,
    sib_out,
    sib_in,
    total,
    rank_out,
    rank_in,
    lifted,
    back,
    w_sem,
    stage_sem,
    local_sem,
    ids_send,
    ids_recv,
    out_send,
    out_recv,
    pair_send,
    pair_recv,
    far_send,
    far_recv,
    sib_send,
    sib_recv,
    rank_send,
    rank_recv,
    back_send,
    back_recv,
):
    me = lax.axis_index("owner")
    t = lax.axis_index("tensor")
    y, core = t // CORES, t % CORES
    chips = tensors // CORES
    sibling = y * CORES + 1 - core
    rows, features = ctx_ref.shape
    per_adapter, _, rank_extent = down_ref.shape
    wide = per_adapter * rank_extent
    slots = outgoing_ref.shape[2]
    block = owners * slots

    barrier = pltpu.get_barrier_semaphore()
    for d in range(1, owners):
        pl.semaphore_signal(
            barrier, inc=1, device_id={"owner": lax.rem(me + d, owners)}, device_id_type=MESH
        )
    for d in range(1, tensors):
        pl.semaphore_signal(
            barrier, inc=1, device_id={"tensor": lax.rem(t + d, tensors)}, device_id_type=MESH
        )
    pl.semaphore_wait(barrier, owners + tensors - 2)

    def ids_copy(d, at):
        to = lax.rem(me + d, owners)
        return remote(
            ids_out_ref.at[to], ids_in.at[at], ids_send.at[d - 1], ids_recv.at[d - 1], "owner", to
        )

    def rows_copy(c, d, at):
        to = lax.rem(me + d, owners)
        return remote(
            outgoing_ref.at[c, to],
            arrived.at[c, at],
            out_send.at[c, d - 1],
            out_recv.at[c, d - 1],
            "owner",
            to,
        )

    def back_copy(c, d, at):
        to = lax.rem(me + d, owners)
        return remote(
            lifted.at[c, to], back.at[c, at], back_send.at[c, d - 1], back_recv.at[c, d - 1], "owner", to
        )

    def source(d):
        return lax.rem(me - d + owners, owners)

    for d in range(1, owners):
        ids_copy(d, me).start()
    for c in range(CHUNKS):
        for d in range(1, owners):
            rows_copy(c, d, me).start()

    locals_ = [pltpu.make_async_copy(up_ref, up, local_sem.at[0])]
    locals_.append(pltpu.make_async_copy(ids_out_ref.at[me], ids_in.at[me], local_sem.at[1]))
    for c in range(CHUNKS):
        locals_.append(
            pltpu.make_async_copy(outgoing_ref.at[c, me], arrived.at[c, me], local_sem.at[2 + c])
        )
    for copy in locals_:
        copy.start()

    steps = features // tile
    others = [lax.rem(y + 1 + k, chips) for k in range(chips - 1)]
    order = [o * CORES + 1 - core for o in others]
    order += [o * CORES + core for o in others]
    order += [sibling, t]

    def fetch(column, slot):
        return pltpu.make_async_copy(
            w_ref.at[:, pl.ds(pl.multiple_of(column, tile), tile)], wbuf.at[slot], w_sem.at[slot]
        )

    def product(p, store):
        first = order[p] * features
        after = order[p + 1] * features if p + 1 < tensors else None

        def body(j, carry):
            slot = lax.rem(p * steps + j, 2)
            if after is not None:
                fetch(jnp.where(j + 1 < steps, first + (j + 1) * tile, after), 1 - slot).start()
            else:

                @pl.when(j + 1 < steps)
                def _():
                    fetch(first + (j + 1) * tile, 1 - slot).start()

            fetch(first + j * tile, slot).wait()
            store(
                pl.ds(pl.multiple_of(j * tile, tile), tile),
                jnp.dot(ctx_ref[...], wbuf[slot], preferred_element_type=F32).astype(BF16),
            )
            return carry

        lax.fori_loop(0, steps, body, 0)

    def pair_copy(k):
        return remote(
            pair_out.at[k], pair_in.at[k], pair_send.at[k], pair_recv.at[k], "tensor", sibling
        )

    def far_copy(k):
        return remote(
            far_out.at[k],
            far_in.at[k],
            far_send.at[k],
            far_recv.at[k],
            "tensor",
            others[k] * CORES + core,
        )

    def sib_copy():
        return remote(sib_out, sib_in, sib_send, sib_recv, "tensor", sibling)

    fetch(order[0] * features, 0).start()
    for k in range(chips - 1):

        def keep_pair(columns, value, k=k):
            pair_out[k, :, columns] = value

        product(k, keep_pair)
        pair_copy(k).start()
    for k in range(chips - 1):
        pair_copy(k).wait_recv()

        def keep_far(columns, value, k=k):
            far_out[k, :, columns] = (
                value.astype(F32) + pair_in[k, :, columns].astype(F32)
            ).astype(BF16)

        product(chips - 1 + k, keep_far)
        far_copy(k).start()

    def keep_sib(columns, value):
        sib_out[:, columns] = value

    product(tensors - 2, keep_sib)
    sib_copy().start()

    def keep_own(columns, value):
        total[:, columns] = value.astype(F32)

    product(tensors - 1, keep_own)

    def stage_copy(j, half, slot):
        return pltpu.make_async_copy(
            down_ref.at[2 * j + half], stage.at[slot, half], stage_sem.at[slot, half]
        )

    pairs = per_adapter // 2
    for half in range(2):
        stage_copy(0, half, 0).start()

    def lay(j, carry):
        slot = lax.rem(j, 2)

        @pl.when(j + 1 < pairs)
        def _():
            for half in range(2):
                stage_copy(j + 1, half, 1 - slot).start()

        for half in range(2):
            stage_copy(j, half, slot).wait()
        down[:, pl.ds(pl.multiple_of(j * 2 * rank_extent, 2 * rank_extent), 2 * rank_extent)] = (
            jnp.concatenate([stage[slot, 0], stage[slot, 1]], axis=1)
        )
        return carry

    lax.fori_loop(0, pairs, lay, 0)

    for copy in locals_:
        copy.wait()
    for d in range(1, owners):
        ids_copy(d, source(d)).wait_recv()

    lanes = 2 * rank_extent
    pick = (
        lax.broadcasted_iota(jnp.int32, (wide, lanes), 0) % rank_extent
        == lax.broadcasted_iota(jnp.int32, (wide, lanes), 1)
    ).astype(F32).astype(BF16)
    eye = lax.broadcasted_iota(jnp.int32, (slots, slots), 0) == lax.broadcasted_iota(
        jnp.int32, (slots, slots), 1
    )
    block_of = lax.broadcasted_iota(jnp.int32, (slots, wide), 1) // rank_extent

    def mask_of(c, s):
        numbers = ids_in[s, 0:1, c * slots : (c + 1) * slots]
        column = jnp.sum(jnp.where(eye, numbers.astype(F32), 0.0), axis=1, keepdims=True)
        return column.astype(jnp.int32) == block_of

    def rank_copy(c, d):
        to = lax.rem(t + d, tensors)
        return remote(
            rank_out.at[c],
            rank_in.at[c, d - 1],
            rank_send.at[c, d - 1],
            rank_recv.at[c, d - 1],
            "tensor",
            to,
        )

    def reduce_chunk(c):
        for d in range(1, owners):
            rows_copy(c, d, source(d)).wait_recv()
        full = jnp.dot(
            arrived[c].reshape(block, features), down[...], preferred_element_type=F32
        )
        for s in range(owners):
            mine = slice(s * slots, (s + 1) * slots)
            held = jnp.where(mask_of(c, s), full[mine], 0.0).astype(BF16)
            rank_out[c, mine] = jnp.dot(held, pick, preferred_element_type=F32).astype(BF16)
        for d in range(1, tensors):
            rank_copy(c, d).start()

    def lift_chunk(c):
        for d in range(1, tensors):
            rank_copy(c, d).wait_recv()
        reduced = rank_out[c].astype(F32)
        for d in range(1, tensors):
            reduced = reduced + rank_in[c, d - 1].astype(F32)
        spread = lax.dot_general(
            reduced.astype(BF16), pick, (((1,), (1,)), ((), ())), preferred_element_type=F32
        )
        held = jnp.concatenate(
            [
                jnp.where(mask_of(c, s), spread[s * slots : (s + 1) * slots], 0.0).astype(BF16)
                for s in range(owners)
            ],
            axis=0,
        )
        lifted[c] = (
            jnp.dot(held, up[...], preferred_element_type=F32)
            .astype(BF16)
            .reshape(owners, slots, features)
        )
        for d in range(1, owners):
            back_copy(c, d, me).start()
        back[c, me] = lifted[c, me]

    for c in range(CHUNKS):
        reduce_chunk(c)
        lift_chunk(c)

    sib_copy().wait_recv()
    total[...] += sib_in[...].astype(F32)
    for k in range(chips - 1):
        far_copy(k).wait_recv()
        total[...] += far_in[k].astype(F32)

    for c in range(CHUNKS):
        for d in range(1, owners):
            back_copy(c, d, source(d)).wait_recv()
        sum_ = total[...] + jnp.dot(
            place_ref[c], back[c].reshape(block, features), preferred_element_type=F32
        )
        if c + 1 < CHUNKS:
            total[...] = sum_
        else:
            out_ref[...] = sum_.astype(BF16)

    for d in range(1, owners):
        ids_copy(d, me).wait_send()
        for c in range(CHUNKS):
            rows_copy(c, d, me).wait_send()
            back_copy(c, d, me).wait_send()
    for k in range(chips - 1):
        pair_copy(k).wait_send()
        far_copy(k).wait_send()
    sib_copy().wait_send()
    for c in range(CHUNKS):
        for d in range(1, tensors):
            rank_copy(c, d).wait_send()


def on_device(context, output_weight, adapter_down, adapter_up, token_adapter):
    owners = lax.axis_size("owner")
    tensors = lax.axis_size("tensor")
    tokens, features = context.shape
    per_adapter, _, rank_extent = adapter_down.shape
    slots = tokens // 2 // CHUNKS
    wide = per_adapter * rank_extent
    tile = min(512, features)
    chips = tensors // CORES

    target = token_adapter // per_adapter
    within = token_adapter % per_adapter
    onehot = (target[:, None] == jnp.arange(owners)[None, :]).astype(BF16)
    before = (jnp.arange(tokens)[:, None] > jnp.arange(tokens)[None, :]).astype(BF16)
    counts = jnp.dot(before, onehot, preferred_element_type=F32)
    rank = jnp.sum(counts * onehot.astype(F32), axis=1).astype(jnp.int32)
    slot = (rank // slots * owners + target) * slots + rank % slots
    hit = slot[:, None] == jnp.arange(CHUNKS * owners * slots)[None, :]
    place = hit.astype(BF16)
    outgoing = (
        lax.dot_general(place, context, (((0,), (0,)), ((), ())), preferred_element_type=F32)
        .astype(BF16)
        .reshape(CHUNKS, owners, slots, features)
    )
    ids = jnp.max(jnp.where(hit, within[:, None], -1), axis=0).reshape(CHUNKS, owners, slots)
    ids = ids.transpose(1, 0, 2).reshape(owners, 1, CHUNKS * slots)
    ids = jnp.broadcast_to(ids, (owners, 8, CHUNKS * slots))
    place = place.reshape(tokens, CHUNKS, owners * slots).transpose(1, 0, 2)

    anywhere = pl.BlockSpec(memory_space=pl.ANY)
    vmem = pl.BlockSpec(memory_space=pltpu.VMEM)
    dma = pltpu.SemaphoreType.DMA
    return pl.pallas_call(
        functools.partial(kernel, owners, tensors, tile),
        out_shape=jax.ShapeDtypeStruct((tokens, features), BF16),
        in_specs=[vmem, anywhere, anywhere, anywhere, anywhere, anywhere, vmem],
        out_specs=vmem,
        scratch_shapes=[
            pltpu.VMEM((CHUNKS, owners, slots, features), BF16),
            pltpu.VMEM((owners, 8, CHUNKS * slots), jnp.int32),
            pltpu.VMEM((2, 2, features, rank_extent), BF16),
            pltpu.VMEM((features, wide), BF16),
            pltpu.VMEM((wide, features), BF16),
            pltpu.VMEM((2, features, tile), BF16),
            pltpu.VMEM((chips - 1, tokens, features), BF16),
            pltpu.VMEM((chips - 1, tokens, features), BF16),
            pltpu.VMEM((chips - 1, tokens, features), BF16),
            pltpu.VMEM((chips - 1, tokens, features), BF16),
            pltpu.VMEM((tokens, features), BF16),
            pltpu.VMEM((tokens, features), BF16),
            pltpu.VMEM((tokens, features), F32),
            pltpu.VMEM((CHUNKS, owners * slots, 2 * rank_extent), BF16),
            pltpu.VMEM((CHUNKS, tensors - 1, owners * slots, 2 * rank_extent), BF16),
            pltpu.VMEM((CHUNKS, owners, slots, features), BF16),
            pltpu.VMEM((CHUNKS, owners, slots, features), BF16),
            dma((2,)),
            dma((2, 2)),
            dma((2 + CHUNKS,)),
            dma((owners - 1,)),
            dma((owners - 1,)),
            dma((CHUNKS, owners - 1)),
            dma((CHUNKS, owners - 1)),
            dma((chips - 1,)),
            dma((chips - 1,)),
            dma((chips - 1,)),
            dma((chips - 1,)),
            dma,
            dma,
            dma((CHUNKS, tensors - 1)),
            dma((CHUNKS, tensors - 1)),
            dma((CHUNKS, owners - 1)),
            dma((CHUNKS, owners - 1)),
        ],
        compiler_params=pltpu.CompilerParams(
            collective_id=0, has_side_effects=True, vmem_limit_bytes=60 * 1024 * 1024
        ),
        cost_estimate=pl.CostEstimate(
            flops=2 * tokens * features * features * tensors,
            bytes_accessed=2 * features * features * tensors,
            transcendentals=0,
        ),
    )(
        context,
        output_weight,
        adapter_down,
        adapter_up.reshape(wide, features),
        outgoing,
        ids,
        place,
    )


def solution(mesh):
    placed = (
        P(("replica", "owner"), "tensor"),
        P("tensor", None),
        P("owner", "tensor", None),
        P("owner", None, "tensor"),
        P(("replica", "owner")),
    )
    return jax.shard_map(
        on_device,
        mesh=mesh,
        in_specs=placed,
        out_specs=P(("replica", "owner"), "tensor"),
        check_vma=False,
    )
```

```python
import functools

import jax
import jax.numpy as jnp
from jax import lax
from jax.experimental import pallas as pl
from jax.experimental.pallas import tpu as pltpu
from jax.sharding import PartitionSpec as P

BF16 = jnp.bfloat16
F32 = jnp.float32
MESH = pl.DeviceIdType.MESH
CORES = 2
CHUNKS = 2


def remote(src, dst, send, recv, axis, index):
    return pltpu.make_async_remote_copy(
        src_ref=src,
        dst_ref=dst,
        send_sem=send,
        recv_sem=recv,
        device_id={axis: index},
        device_id_type=MESH,
    )


def kernel(
    owners,
    tensors,
    tile,
    rank_extent,
    ctx_ref,
    w_ref,
    down_ref,
    up_ref,
    ids_out_ref,
    place_ref,
    out_ref,
    outgoing,
    arrived,
    ids_in,
    down,
    up,
    wbuf,
    pair_out,
    pair_in,
    far_out,
    far_in,
    sib_out,
    sib_in,
    total,
    rank_out,
    rank_in,
    lifted,
    back,
    w_sem,
    local_sem,
    ids_send,
    ids_recv,
    out_send,
    out_recv,
    pair_send,
    pair_recv,
    far_send,
    far_recv,
    sib_send,
    sib_recv,
    rank_send,
    rank_recv,
    back_send,
    back_recv,
):
    me = lax.axis_index("owner")
    t = lax.axis_index("tensor")
    y, core = t // CORES, t % CORES
    chips = tensors // CORES
    sibling = y * CORES + 1 - core
    rows, features = ctx_ref.shape
    wide = down_ref.shape[0]
    slots = place_ref.shape[2] // owners
    block = owners * slots

    barrier = pltpu.get_barrier_semaphore()
    for d in range(1, owners):
        pl.semaphore_signal(
            barrier, inc=1, device_id={"owner": lax.rem(me + d, owners)}, device_id_type=MESH
        )
    for d in range(1, tensors):
        pl.semaphore_signal(
            barrier, inc=1, device_id={"tensor": lax.rem(t + d, tensors)}, device_id_type=MESH
        )
    pl.semaphore_wait(barrier, owners + tensors - 2)

    def ids_copy(d, at):
        to = lax.rem(me + d, owners)
        return remote(
            ids_out_ref.at[to], ids_in.at[at], ids_send.at[d - 1], ids_recv.at[d - 1], "owner", to
        )

    def rows_copy(c, d, at):
        to = lax.rem(me + d, owners)
        return remote(
            outgoing.at[c, to],
            arrived.at[c, at],
            out_send.at[c, d - 1],
            out_recv.at[c, d - 1],
            "owner",
            to,
        )

    def back_copy(c, d, at):
        to = lax.rem(me + d, owners)
        return remote(
            lifted.at[c, to], back.at[c, at], back_send.at[c, d - 1], back_recv.at[c, d - 1], "owner", to
        )

    def source(d):
        return lax.rem(me - d + owners, owners)

    for d in range(1, owners):
        ids_copy(d, me).start()

    def chosen(c, to):
        columns = pl.ds(pl.multiple_of(to * slots, slots), slots)
        return lax.dot_general(
            place_ref[c, :, columns],
            ctx_ref[...],
            (((0,), (0,)), ((), ())),
            preferred_element_type=F32,
        ).astype(BF16)

    for c in range(CHUNKS):
        for d in range(1, owners):
            to = lax.rem(me + d, owners)
            outgoing[c, to] = chosen(c, to)
            rows_copy(c, d, me).start()

    locals_ = [pltpu.make_async_copy(up_ref, up, local_sem.at[0])]
    locals_.append(pltpu.make_async_copy(ids_out_ref.at[me], ids_in.at[me], local_sem.at[1]))
    locals_.append(pltpu.make_async_copy(down_ref, down, local_sem.at[2]))
    for copy in locals_:
        copy.start()
    for c in range(CHUNKS):
        arrived[c, me] = chosen(c, me)

    steps = features // tile
    others = [lax.rem(y + 1 + k, chips) for k in range(chips - 1)]
    order = [o * CORES + 1 - core for o in others]
    order += [o * CORES + core for o in others]
    order += [sibling, t]

    def fetch(column, slot):
        return pltpu.make_async_copy(
            w_ref.at[:, pl.ds(pl.multiple_of(column, tile), tile)], wbuf.at[slot], w_sem.at[slot]
        )

    def product(p, store):
        first = order[p] * features
        after = order[p + 1] * features if p + 1 < tensors else None

        def body(j, carry):
            slot = lax.rem(p * steps + j, 2)
            if after is not None:
                fetch(jnp.where(j + 1 < steps, first + (j + 1) * tile, after), 1 - slot).start()
            else:

                @pl.when(j + 1 < steps)
                def _():
                    fetch(first + (j + 1) * tile, 1 - slot).start()

            fetch(first + j * tile, slot).wait()
            store(
                pl.ds(pl.multiple_of(j * tile, tile), tile),
                jnp.dot(ctx_ref[...], wbuf[slot], preferred_element_type=F32).astype(BF16),
            )
            return carry

        lax.fori_loop(0, steps, body, 0)

    def pair_copy(k):
        return remote(
            pair_out.at[k], pair_in.at[k], pair_send.at[k], pair_recv.at[k], "tensor", sibling
        )

    def far_copy(k):
        return remote(
            far_out.at[k],
            far_in.at[k],
            far_send.at[k],
            far_recv.at[k],
            "tensor",
            others[k] * CORES + core,
        )

    def sib_copy():
        return remote(sib_out, sib_in, sib_send, sib_recv, "tensor", sibling)

    fetch(order[0] * features, 0).start()
    for k in range(chips - 1):

        def keep_pair(columns, value, k=k):
            pair_out[k, :, columns] = value

        product(k, keep_pair)
        pair_copy(k).start()
    for k in range(chips - 1):
        pair_copy(k).wait_recv()

        def keep_far(columns, value, k=k):
            far_out[k, :, columns] = (
                value.astype(F32) + pair_in[k, :, columns].astype(F32)
            ).astype(BF16)

        product(chips - 1 + k, keep_far)
        far_copy(k).start()

    def keep_sib(columns, value):
        sib_out[:, columns] = value

    product(tensors - 2, keep_sib)
    sib_copy().start()

    def keep_own(columns, value):
        total[:, columns] = value.astype(F32)

    product(tensors - 1, keep_own)

    for copy in locals_:
        copy.wait()
    for d in range(1, owners):
        ids_copy(d, source(d)).wait_recv()

    lanes = 2 * rank_extent
    pick = (
        lax.broadcasted_iota(jnp.int32, (wide, lanes), 0) % rank_extent
        == lax.broadcasted_iota(jnp.int32, (wide, lanes), 1)
    ).astype(F32).astype(BF16)
    eye = lax.broadcasted_iota(jnp.int32, (slots, slots), 0) == lax.broadcasted_iota(
        jnp.int32, (slots, slots), 1
    )
    block_of = lax.broadcasted_iota(jnp.int32, (slots, wide), 1) // rank_extent

    def mask_of(c, s):
        numbers = ids_in[s, 0:1, c * slots : (c + 1) * slots]
        column = jnp.sum(jnp.where(eye, numbers.astype(F32), 0.0), axis=1, keepdims=True)
        return column.astype(jnp.int32) == block_of

    def rank_copy(c, d):
        to = lax.rem(t + d, tensors)
        return remote(
            rank_out.at[c],
            rank_in.at[c, d - 1],
            rank_send.at[c, d - 1],
            rank_recv.at[c, d - 1],
            "tensor",
            to,
        )

    def reduce_chunk(c):
        for d in range(1, owners):
            rows_copy(c, d, source(d)).wait_recv()
        full = lax.dot_general(
            arrived[c].reshape(block, features),
            down[...],
            (((1,), (1,)), ((), ())),
            preferred_element_type=F32,
        )
        for s in range(owners):
            mine = slice(s * slots, (s + 1) * slots)
            held = jnp.where(mask_of(c, s), full[mine], 0.0).astype(BF16)
            rank_out[c, mine] = jnp.dot(held, pick, preferred_element_type=F32).astype(BF16)
        for d in range(1, tensors):
            rank_copy(c, d).start()

    def lift_chunk(c):
        for d in range(1, tensors):
            rank_copy(c, d).wait_recv()
        reduced = rank_out[c].astype(F32)
        for d in range(1, tensors):
            reduced = reduced + rank_in[c, d - 1].astype(F32)
        spread = lax.dot_general(
            reduced.astype(BF16), pick, (((1,), (1,)), ((), ())), preferred_element_type=F32
        )
        held = jnp.concatenate(
            [
                jnp.where(mask_of(c, s), spread[s * slots : (s + 1) * slots], 0.0).astype(BF16)
                for s in range(owners)
            ],
            axis=0,
        )
        lifted[c] = (
            jnp.dot(held, up[...], preferred_element_type=F32)
            .astype(BF16)
            .reshape(owners, slots, features)
        )
        for d in range(1, owners):
            back_copy(c, d, me).start()
        back[c, me] = lifted[c, me]

    for c in range(CHUNKS):
        reduce_chunk(c)
        lift_chunk(c)

    sib_copy().wait_recv()
    total[...] += sib_in[...].astype(F32)
    for k in range(chips - 1):
        far_copy(k).wait_recv()
        total[...] += far_in[k].astype(F32)

    for c in range(CHUNKS):
        for d in range(1, owners):
            back_copy(c, d, source(d)).wait_recv()
        sum_ = total[...] + jnp.dot(
            place_ref[c], back[c].reshape(block, features), preferred_element_type=F32
        )
        if c + 1 < CHUNKS:
            total[...] = sum_
        else:
            out_ref[...] = sum_.astype(BF16)

    for d in range(1, owners):
        ids_copy(d, me).wait_send()
        for c in range(CHUNKS):
            rows_copy(c, d, me).wait_send()
            back_copy(c, d, me).wait_send()
    for k in range(chips - 1):
        pair_copy(k).wait_send()
        far_copy(k).wait_send()
    sib_copy().wait_send()
    for c in range(CHUNKS):
        for d in range(1, tensors):
            rank_copy(c, d).wait_send()


def on_device(context, output_weight, adapter_down, adapter_up, token_adapter):
    owners = lax.axis_size("owner")
    tensors = lax.axis_size("tensor")
    tokens, features = context.shape
    per_adapter, _, rank_extent = adapter_down.shape
    slots = tokens // 2 // CHUNKS
    wide = per_adapter * rank_extent
    tile = min(512, features)
    chips = tensors // CORES

    target = token_adapter // per_adapter
    within = token_adapter % per_adapter
    onehot = (target[:, None] == jnp.arange(owners)[None, :]).astype(BF16)
    before = (jnp.arange(tokens)[:, None] > jnp.arange(tokens)[None, :]).astype(BF16)
    counts = jnp.dot(before, onehot, preferred_element_type=F32)
    rank = jnp.sum(counts * onehot.astype(F32), axis=1).astype(jnp.int32)
    slot = (rank // slots * owners + target) * slots + rank % slots
    hit = slot[:, None] == jnp.arange(CHUNKS * owners * slots)[None, :]
    place = hit.astype(BF16)
    ids = jnp.max(jnp.where(hit, within[:, None], -1), axis=0).reshape(CHUNKS, owners, slots)
    ids = ids.transpose(1, 0, 2).reshape(owners, 1, CHUNKS * slots)
    ids = jnp.broadcast_to(ids, (owners, 8, CHUNKS * slots))
    place = place.reshape(tokens, CHUNKS, owners * slots).transpose(1, 0, 2)

    anywhere = pl.BlockSpec(memory_space=pl.ANY)
    vmem = pl.BlockSpec(memory_space=pltpu.VMEM)
    dma = pltpu.SemaphoreType.DMA
    return pl.pallas_call(
        functools.partial(kernel, owners, tensors, tile, rank_extent),
        out_shape=jax.ShapeDtypeStruct((tokens, features), BF16),
        in_specs=[vmem, anywhere, anywhere, anywhere, anywhere, vmem],
        out_specs=vmem,
        scratch_shapes=[
            pltpu.VMEM((CHUNKS, owners, slots, features), BF16),
            pltpu.VMEM((CHUNKS, owners, slots, features), BF16),
            pltpu.VMEM((owners, 8, CHUNKS * slots), jnp.int32),
            pltpu.VMEM((wide, features), BF16),
            pltpu.VMEM((wide, features), BF16),
            pltpu.VMEM((2, features, tile), BF16),
            pltpu.VMEM((chips - 1, tokens, features), BF16),
            pltpu.VMEM((chips - 1, tokens, features), BF16),
            pltpu.VMEM((chips - 1, tokens, features), BF16),
            pltpu.VMEM((chips - 1, tokens, features), BF16),
            pltpu.VMEM((tokens, features), BF16),
            pltpu.VMEM((tokens, features), BF16),
            pltpu.VMEM((tokens, features), F32),
            pltpu.VMEM((CHUNKS, owners * slots, 2 * rank_extent), BF16),
            pltpu.VMEM((CHUNKS, tensors - 1, owners * slots, 2 * rank_extent), BF16),
            pltpu.VMEM((CHUNKS, owners, slots, features), BF16),
            pltpu.VMEM((CHUNKS, owners, slots, features), BF16),
            dma((2,)),
            dma((3,)),
            dma((owners - 1,)),
            dma((owners - 1,)),
            dma((CHUNKS, owners - 1)),
            dma((CHUNKS, owners - 1)),
            dma((chips - 1,)),
            dma((chips - 1,)),
            dma((chips - 1,)),
            dma((chips - 1,)),
            dma,
            dma,
            dma((CHUNKS, tensors - 1)),
            dma((CHUNKS, tensors - 1)),
            dma((CHUNKS, owners - 1)),
            dma((CHUNKS, owners - 1)),
        ],
        compiler_params=pltpu.CompilerParams(
            collective_id=0, has_side_effects=True, vmem_limit_bytes=60 * 1024 * 1024
        ),
        cost_estimate=pl.CostEstimate(
            flops=2 * tokens * features * features * tensors,
            bytes_accessed=2 * features * features * tensors,
            transcendentals=0,
        ),
    )(
        context,
        output_weight,
        adapter_down.transpose(0, 2, 1).reshape(wide, features),
        adapter_up.reshape(wide, features),
        ids,
        place,
    )


def solution(mesh):
    placed = (
        P(("replica", "owner"), "tensor"),
        P("tensor", None),
        P("owner", "tensor", None),
        P("owner", None, "tensor"),
        P(("replica", "owner")),
    )
    return jax.shard_map(
        on_device,
        mesh=mesh,
        in_specs=placed,
        out_specs=P(("replica", "owner"), "tensor"),
        check_vma=False,
    )
```

```python
import functools

import jax
import jax.numpy as jnp
from jax import lax
from jax.experimental import pallas as pl
from jax.experimental.pallas import tpu as pltpu
from jax.sharding import PartitionSpec as P

BF16 = jnp.bfloat16
F32 = jnp.float32
MESH = pl.DeviceIdType.MESH
CORES = 2
CHUNKS = 2


def remote(src, dst, send, recv, axis, index):
    return pltpu.make_async_remote_copy(
        src_ref=src,
        dst_ref=dst,
        send_sem=send,
        recv_sem=recv,
        device_id={axis: index},
        device_id_type=MESH,
    )


def kernel(
    owners,
    tensors,
    tile,
    rank_extent,
    ctx_ref,
    w_ref,
    down_ref,
    up_ref,
    ids_out_ref,
    place_ref,
    out_ref,
    outgoing,
    arrived,
    ids_in,
    down,
    up,
    wbuf,
    pair_out,
    pair_in,
    far_out,
    far_in,
    sib_out,
    sib_in,
    total,
    rank_out,
    rank_in,
    lifted,
    back,
    w_sem,
    local_sem,
    ids_send,
    ids_recv,
    out_send,
    out_recv,
    pair_send,
    pair_recv,
    far_send,
    far_recv,
    sib_send,
    sib_recv,
    rank_send,
    rank_recv,
    back_send,
    back_recv,
):
    me = lax.axis_index("owner")
    t = lax.axis_index("tensor")
    y, core = t // CORES, t % CORES
    chips = tensors // CORES
    sibling = y * CORES + 1 - core
    rows, features = ctx_ref.shape
    wide = down_ref.shape[0]
    slots = place_ref.shape[2] // owners
    block = owners * slots

    barrier = pltpu.get_barrier_semaphore()
    for d in range(1, owners):
        pl.semaphore_signal(
            barrier, inc=1, device_id={"owner": lax.rem(me + d, owners)}, device_id_type=MESH
        )
    for d in range(1, tensors):
        pl.semaphore_signal(
            barrier, inc=1, device_id={"tensor": lax.rem(t + d, tensors)}, device_id_type=MESH
        )
    pl.semaphore_wait(barrier, owners + tensors - 2)

    def ids_copy(d, at):
        to = lax.rem(me + d, owners)
        return remote(
            ids_out_ref.at[to], ids_in.at[at], ids_send.at[d - 1], ids_recv.at[d - 1], "owner", to
        )

    def rows_copy(c, d, at):
        to = lax.rem(me + d, owners)
        return remote(
            outgoing.at[c, to],
            arrived.at[c, at],
            out_send.at[c, d - 1],
            out_recv.at[c, d - 1],
            "owner",
            to,
        )

    def back_copy(c, d, at):
        to = lax.rem(me + d, owners)
        return remote(
            lifted.at[c, to], back.at[c, at], back_send.at[c, d - 1], back_recv.at[c, d - 1], "owner", to
        )

    def source(d):
        return lax.rem(me - d + owners, owners)

    for d in range(1, owners):
        ids_copy(d, me).start()

    def chosen(c, to):
        columns = pl.ds(pl.multiple_of(to * slots, slots), slots)
        return lax.dot_general(
            place_ref[c, :, columns],
            ctx_ref[...],
            (((0,), (0,)), ((), ())),
            preferred_element_type=F32,
        ).astype(BF16)

    for c in range(CHUNKS):
        for d in range(1, owners):
            to = lax.rem(me + d, owners)
            outgoing[c, to] = chosen(c, to)
            rows_copy(c, d, me).start()

    locals_ = [pltpu.make_async_copy(up_ref, up, local_sem.at[0])]
    locals_.append(pltpu.make_async_copy(ids_out_ref.at[me], ids_in.at[me], local_sem.at[1]))
    locals_.append(pltpu.make_async_copy(down_ref, down, local_sem.at[2]))
    for copy in locals_:
        copy.start()
    for c in range(CHUNKS):
        arrived[c, me] = chosen(c, me)

    steps = features // tile
    others = [lax.rem(y + 1 + k, chips) for k in range(chips - 1)]
    order = [o * CORES + 1 - core for o in others]
    order += [o * CORES + core for o in others]
    order += [sibling, t]

    def fetch(column, slot):
        return pltpu.make_async_copy(
            w_ref.at[:, pl.ds(pl.multiple_of(column, tile), tile)], wbuf.at[slot], w_sem.at[slot]
        )

    def product(p, store):
        first = order[p] * features
        after = order[p + 1] * features if p + 1 < tensors else None

        def body(j, carry):
            slot = lax.rem(p * steps + j, 2)
            if after is not None:
                fetch(jnp.where(j + 1 < steps, first + (j + 1) * tile, after), 1 - slot).start()
            else:

                @pl.when(j + 1 < steps)
                def _():
                    fetch(first + (j + 1) * tile, 1 - slot).start()

            fetch(first + j * tile, slot).wait()
            store(
                pl.ds(pl.multiple_of(j * tile, tile), tile),
                jnp.dot(ctx_ref[...], wbuf[slot], preferred_element_type=F32).astype(BF16),
            )
            return carry

        lax.fori_loop(0, steps, body, 0)

    def pair_copy(k):
        return remote(
            pair_out.at[k], pair_in.at[k], pair_send.at[k], pair_recv.at[k], "tensor", sibling
        )

    def far_copy(k):
        return remote(
            far_out.at[k],
            far_in.at[k],
            far_send.at[k],
            far_recv.at[k],
            "tensor",
            others[k] * CORES + core,
        )

    def sib_copy():
        return remote(sib_out, sib_in, sib_send, sib_recv, "tensor", sibling)

    fetch(order[0] * features, 0).start()
    for k in range(chips - 1):

        def keep_pair(columns, value, k=k):
            pair_out[k, :, columns] = value

        product(k, keep_pair)
        pair_copy(k).start()
    for k in range(chips - 1):
        pair_copy(k).wait_recv()

        def keep_far(columns, value, k=k):
            far_out[k, :, columns] = (
                value.astype(F32) + pair_in[k, :, columns].astype(F32)
            ).astype(BF16)

        product(chips - 1 + k, keep_far)
        far_copy(k).start()

    def keep_sib(columns, value):
        sib_out[:, columns] = value

    product(tensors - 2, keep_sib)
    sib_copy().start()

    def keep_own(columns, value):
        total[:, columns] = value.astype(F32)

    product(tensors - 1, keep_own)

    for copy in locals_:
        copy.wait()
    for d in range(1, owners):
        ids_copy(d, source(d)).wait_recv()

    lanes = 2 * rank_extent
    pick = (
        lax.broadcasted_iota(jnp.int32, (wide, lanes), 0) % rank_extent
        == lax.broadcasted_iota(jnp.int32, (wide, lanes), 1)
    ).astype(F32).astype(BF16)
    eye = lax.broadcasted_iota(jnp.int32, (slots, slots), 0) == lax.broadcasted_iota(
        jnp.int32, (slots, slots), 1
    )
    block_of = lax.broadcasted_iota(jnp.int32, (slots, wide), 1) // rank_extent

    def mask_of(c, s):
        numbers = ids_in[s, 0:1, c * slots : (c + 1) * slots]
        column = jnp.sum(jnp.where(eye, numbers.astype(F32), 0.0), axis=1, keepdims=True)
        return column.astype(jnp.int32) == block_of

    def rank_copy(c, d):
        to = lax.rem(t + d, tensors)
        return remote(
            rank_out.at[c],
            rank_in.at[c, d - 1],
            rank_send.at[c, d - 1],
            rank_recv.at[c, d - 1],
            "tensor",
            to,
        )

    def reduce_chunk(c):
        for d in range(1, owners):
            rows_copy(c, d, source(d)).wait_recv()
        full = lax.dot_general(
            arrived[c].reshape(block, features),
            down[...],
            (((1,), (1,)), ((), ())),
            preferred_element_type=F32,
        )
        for s in range(owners):
            mine = slice(s * slots, (s + 1) * slots)
            held = jnp.where(mask_of(c, s), full[mine], 0.0).astype(BF16)
            rank_out[c, mine] = jnp.dot(held, pick, preferred_element_type=F32).astype(BF16)
        for d in range(1, tensors):
            rank_copy(c, d).start()

    def lift_chunk(c):
        for d in range(1, tensors):
            rank_copy(c, d).wait_recv()
        reduced = rank_out[c].astype(F32)
        for d in range(1, tensors):
            reduced = reduced + rank_in[c, d - 1].astype(F32)
        spread = lax.dot_general(
            reduced.astype(BF16), pick, (((1,), (1,)), ((), ())), preferred_element_type=F32
        )
        held = jnp.concatenate(
            [
                jnp.where(mask_of(c, s), spread[s * slots : (s + 1) * slots], 0.0).astype(BF16)
                for s in range(owners)
            ],
            axis=0,
        )
        lifted[c] = (
            jnp.dot(held, up[...], preferred_element_type=F32)
            .astype(BF16)
            .reshape(owners, slots, features)
        )
        for d in range(1, owners):
            back_copy(c, d, me).start()
        back[c, me] = lifted[c, me]

    for c in range(CHUNKS):
        reduce_chunk(c)
        lift_chunk(c)

    sib_copy().wait_recv()
    total[...] += sib_in[...].astype(F32)
    for k in range(chips - 1):
        far_copy(k).wait_recv()
        total[...] += far_in[k].astype(F32)

    for c in range(CHUNKS):
        for d in range(1, owners):
            back_copy(c, d, source(d)).wait_recv()
        sum_ = total[...] + jnp.dot(
            place_ref[c], back[c].reshape(block, features), preferred_element_type=F32
        )
        if c + 1 < CHUNKS:
            total[...] = sum_
        else:
            out_ref[...] = sum_.astype(BF16)

    for d in range(1, owners):
        ids_copy(d, me).wait_send()
        for c in range(CHUNKS):
            rows_copy(c, d, me).wait_send()
            back_copy(c, d, me).wait_send()
    for k in range(chips - 1):
        pair_copy(k).wait_send()
        far_copy(k).wait_send()
    sib_copy().wait_send()
    for c in range(CHUNKS):
        for d in range(1, tensors):
            rank_copy(c, d).wait_send()


def fast_kernel(
    owners,
    tensors,
    tile,
    rank_extent,
    ctx_ref,
    w_ref,
    down_ref,
    up_ref,
    ids_out_ref,
    place_ref,
    extra_ref,
    out_ref,
    flag_ref,
    outgoing,
    arrived,
    ids_in,
    down,
    up,
    wbuf,
    pair_out,
    pair_in,
    far_out,
    far_in,
    sib_out,
    sib_in,
    total,
    rank_out,
    rank_in,
    lifted,
    back,
    w_sem,
    local_sem,
    ids_send,
    ids_recv,
    out_send,
    out_recv,
    pair_send,
    pair_recv,
    far_send,
    far_recv,
    sib_send,
    sib_recv,
    rank_send,
    rank_recv,
    back_send,
    back_recv,
    sums_in,
    flags,
    extra_send,
    extra_recv,
    sums_send,
    sums_recv,
    flag_send,
    flag_recv,
):
    me = lax.axis_index("owner")
    t = lax.axis_index("tensor")
    y, core = t // CORES, t % CORES
    chips = tensors // CORES
    sibling = y * CORES + 1 - core
    rows, features = ctx_ref.shape
    wide = down_ref.shape[0]
    slots = place_ref.shape[2] // owners
    block = owners * slots

    barrier = pltpu.get_barrier_semaphore()
    for d in range(1, owners):
        pl.semaphore_signal(
            barrier, inc=1, device_id={"owner": lax.rem(me + d, owners)}, device_id_type=MESH
        )
    for d in range(1, tensors):
        pl.semaphore_signal(
            barrier, inc=1, device_id={"tensor": lax.rem(t + d, tensors)}, device_id_type=MESH
        )
    replicas = flags.shape[0]
    part = lax.axis_index("replica")
    for d in range(1, replicas):
        pl.semaphore_signal(
            barrier,
            inc=1,
            device_id={"replica": lax.rem(part + d, replicas)},
            device_id_type=MESH,
        )
    pl.semaphore_wait(barrier, owners + tensors + replicas - 3)

    def ids_copy(d, at):
        to = lax.rem(me + d, owners)
        return remote(
            ids_out_ref.at[to], ids_in.at[at], ids_send.at[d - 1], ids_recv.at[d - 1], "owner", to
        )

    def rows_copy(c, d, at):
        to = lax.rem(me + d, owners)
        return remote(
            outgoing.at[c, to],
            arrived.at[c, at],
            out_send.at[c, d - 1],
            out_recv.at[c, d - 1],
            "owner",
            to,
        )

    def back_copy(c, d, at):
        to = lax.rem(me + d, owners)
        return remote(
            lifted.at[c, to], back.at[c, at], back_send.at[c, d - 1], back_recv.at[c, d - 1], "owner", to
        )

    def source(d):
        return lax.rem(me - d + owners, owners)

    for d in range(1, owners):
        ids_copy(d, me).start()

    def chosen(c, to):
        columns = pl.ds(pl.multiple_of(to * slots, slots), slots)
        return lax.dot_general(
            place_ref[c, :, columns],
            ctx_ref[...],
            (((0,), (0,)), ((), ())),
            preferred_element_type=F32,
        ).astype(BF16)

    def extra_copy(way, s):
        return remote(
            arrived.at[1, s],
            arrived.at[1, s],
            extra_send.at[way, s],
            extra_recv.at[s],
            "owner",
            lax.rem(me + (1 if way else owners - 1), owners),
        )

    def pass_on(s, way):
        @pl.when((me + 1 < owners) if way else (me > 0))
        def _():
            extra_copy(way, s).start()

    arrived[1, me] = lax.dot_general(
        extra_ref[...], ctx_ref[...], (((0,), (0,)), ((), ())), preferred_element_type=F32
    ).astype(BF16)
    pass_on(me, 1)
    pass_on(me, 0)

    for d in range(1, owners):
        to = lax.rem(me + d, owners)
        outgoing[0, to] = chosen(0, to)
        rows_copy(0, d, me).start()

    locals_ = [pltpu.make_async_copy(up_ref, up, local_sem.at[0])]
    locals_.append(pltpu.make_async_copy(ids_out_ref.at[me], ids_in.at[me], local_sem.at[1]))
    locals_.append(pltpu.make_async_copy(down_ref, down, local_sem.at[2]))
    for copy in locals_:
        copy.start()
    arrived[0, me] = chosen(0, me)

    steps = features // tile
    others = [lax.rem(y + 1 + k, chips) for k in range(chips - 1)]
    order = [o * CORES + 1 - core for o in others]
    order += [o * CORES + core for o in others]
    order += [sibling, t]

    def fetch(column, slot):
        return pltpu.make_async_copy(
            w_ref.at[:, pl.ds(pl.multiple_of(column, tile), tile)], wbuf.at[slot], w_sem.at[slot]
        )

    def product(p, store):
        first = order[p] * features
        after = order[p + 1] * features if p + 1 < tensors else None

        def body(j, carry):
            slot = lax.rem(p * steps + j, 2)
            if after is not None:
                fetch(jnp.where(j + 1 < steps, first + (j + 1) * tile, after), 1 - slot).start()
            else:

                @pl.when(j + 1 < steps)
                def _():
                    fetch(first + (j + 1) * tile, 1 - slot).start()

            fetch(first + j * tile, slot).wait()
            store(
                pl.ds(pl.multiple_of(j * tile, tile), tile),
                jnp.dot(ctx_ref[...], wbuf[slot], preferred_element_type=F32).astype(BF16),
            )
            return carry

        lax.fori_loop(0, steps, body, 0)

    def pair_copy(k):
        return remote(
            pair_out.at[k], pair_in.at[k], pair_send.at[k], pair_recv.at[k], "tensor", sibling
        )

    def far_copy(k):
        return remote(
            far_out.at[k],
            far_in.at[k],
            far_send.at[k],
            far_recv.at[k],
            "tensor",
            others[k] * CORES + core,
        )

    def sib_copy():
        return remote(sib_out, sib_in, sib_send, sib_recv, "tensor", sibling)

    fetch(order[0] * features, 0).start()
    for k in range(chips - 1):

        def keep_pair(columns, value, k=k):
            pair_out[k, :, columns] = value

        product(k, keep_pair)
        pair_copy(k).start()
    for k in range(chips - 1):
        pair_copy(k).wait_recv()

        def keep_far(columns, value, k=k):
            far_out[k, :, columns] = (
                value.astype(F32) + pair_in[k, :, columns].astype(F32)
            ).astype(BF16)

        product(chips - 1 + k, keep_far)
        far_copy(k).start()

    def keep_sib(columns, value):
        sib_out[:, columns] = value

    product(tensors - 2, keep_sib)
    sib_copy().start()

    def keep_own(columns, value):
        total[:, columns] = value.astype(F32)

    product(tensors - 1, keep_own)

    for copy in locals_:
        copy.wait()
    for d in range(1, owners):
        ids_copy(d, source(d)).wait_recv()

    lanes = 2 * rank_extent
    pick = (
        lax.broadcasted_iota(jnp.int32, (wide, lanes), 0) % rank_extent
        == lax.broadcasted_iota(jnp.int32, (wide, lanes), 1)
    ).astype(F32).astype(BF16)
    eye = lax.broadcasted_iota(jnp.int32, (slots, slots), 0) == lax.broadcasted_iota(
        jnp.int32, (slots, slots), 1
    )
    block_of = lax.broadcasted_iota(jnp.int32, (slots, wide), 1) // rank_extent

    def mask_of(c, s):
        numbers = ids_in[s, 0:1, c * slots : (c + 1) * slots]
        column = jnp.sum(jnp.where(eye, numbers.astype(F32), 0.0), axis=1, keepdims=True)
        return column.astype(jnp.int32) == block_of

    def rank_copy(c, d):
        to = lax.rem(t + d, tensors)
        return remote(
            rank_out.at[c],
            rank_in.at[c, d - 1],
            rank_send.at[c, d - 1],
            rank_recv.at[c, d - 1],
            "tensor",
            to,
        )

    def reduce_chunk(c):
        if c == 0:
            for d in range(1, owners):
                rows_copy(c, d, source(d)).wait_recv()
        full = lax.dot_general(
            arrived[c].reshape(block, features),
            down[...],
            (((1,), (1,)), ((), ())),
            preferred_element_type=F32,
        )
        for s in range(owners):
            mine = slice(s * slots, (s + 1) * slots)
            held = jnp.where(mask_of(c, s), full[mine], 0.0).astype(BF16)
            rank_out[c, mine] = jnp.dot(held, pick, preferred_element_type=F32).astype(BF16)
        for d in range(1, tensors):
            rank_copy(c, d).start()

    def lift_chunk(c):
        for d in range(1, tensors):
            rank_copy(c, d).wait_recv()
        reduced = rank_out[c].astype(F32)
        for d in range(1, tensors):
            reduced = reduced + rank_in[c, d - 1].astype(F32)
        spread = lax.dot_general(
            reduced.astype(BF16), pick, (((1,), (1,)), ((), ())), preferred_element_type=F32
        )
        held = jnp.concatenate(
            [
                jnp.where(mask_of(c, s), spread[s * slots : (s + 1) * slots], 0.0).astype(BF16)
                for s in range(owners)
            ],
            axis=0,
        )
        lifted[c] = (
            jnp.dot(held, up[...], preferred_element_type=F32)
            .astype(BF16)
            .reshape(owners, slots, features)
        )
        if c == 0:
            for d in range(1, owners):
                back_copy(c, d, me).start()
            back[c, me] = lifted[c, me]

    flag = ids_in[0]
    for s in range(1, owners):
        flag = jnp.maximum(flag, ids_in[s])
    flags[0] = flag

    def flag_copy(d):
        return remote(
            flags.at[0],
            flags.at[d],
            flag_send.at[d - 1],
            flag_recv.at[d - 1],
            "replica",
            lax.rem(part + d, replicas),
        )

    for d in range(1, replicas):
        flag_copy(d).start()

    for k in range(1, owners):
        for way in range(2):
            s = me - k if way else me + k

            @pl.when((s >= 0) if way else (s < owners))
            def _(s=s, way=way):
                extra_copy(way, s).wait_recv()
                pass_on(s, way)

    def sums_copy(way, s):
        return remote(
            lifted.at[1, s],
            sums_in.at[way, s],
            sums_send.at[way, s],
            sums_recv.at[way, s],
            "owner",
            lax.rem(me + (1 if way else owners - 1), owners),
        )

    def add_sum(way, s):
        @pl.when((me > 0) if way else (me + 1 < owners))
        def _():
            sums_copy(way, s).wait_recv()
            lifted[1, s] = lifted[1, s] + sums_in[way, s]

    reduce_chunk(1)
    lift_chunk(1)

    @pl.when(me == 0)
    def _():
        for s in range(owners - 1, 0, -1):
            sums_copy(1, s).start()

    @pl.when(me == owners - 1)
    def _():
        for s in range(owners - 1):
            sums_copy(0, s).start()

    reduce_chunk(0)
    lift_chunk(0)

    for k in range(owners - 1, 0, -1):
        for way in range(2):
            s = me + k if way else me - k
            inside = (s < owners) & (me > 0) if way else (s >= 0) & (me + 1 < owners)

            @pl.when(inside)
            def _(s=s, way=way):
                sums_copy(way, s).wait_recv()
                lifted[1, s] = lifted[1, s] + sums_in[way, s]
                sums_copy(way, s).start()

    sib_copy().wait_recv()
    total[...] += sib_in[...].astype(F32)
    for k in range(chips - 1):
        far_copy(k).wait_recv()
        total[...] += far_in[k].astype(F32)

    for d in range(1, owners):
        back_copy(0, d, source(d)).wait_recv()
    total[...] += jnp.dot(
        place_ref[0], back[0].reshape(block, features), preferred_element_type=F32
    )
    add_sum(0, me)
    add_sum(1, me)
    out_ref[...] = (
        total[...] + jnp.dot(extra_ref[...], lifted[1, me], preferred_element_type=F32)
    ).astype(BF16)

    for d in range(1, replicas):
        flag_copy(d).wait_recv()
    flag = flags[0]
    for d in range(1, replicas):
        flag = jnp.maximum(flag, flags[d])
    flag_ref[...] = flag

    for d in range(1, replicas):
        flag_copy(d).wait_send()
    for way in range(2):
        for s in range(owners):

            @pl.when(((s <= me) & (me + 1 < owners)) if way else ((s >= me) & (me > 0)))
            def _(s=s, way=way):
                extra_copy(way, s).wait_send()

            @pl.when(((s > me) & (me + 1 < owners)) if way else ((s < me) & (me > 0)))
            def _(s=s, way=way):
                sums_copy(way, s).wait_send()
    for d in range(1, owners):
        ids_copy(d, me).wait_send()
        rows_copy(0, d, me).wait_send()
        back_copy(0, d, me).wait_send()
    for k in range(chips - 1):
        pair_copy(k).wait_send()
        far_copy(k).wait_send()
    sib_copy().wait_send()
    for c in range(CHUNKS):
        for d in range(1, tensors):
            rank_copy(c, d).wait_send()


def on_device(context, output_weight, adapter_down, adapter_up, token_adapter):
    owners = lax.axis_size("owner")
    tensors = lax.axis_size("tensor")
    replicas = lax.axis_size("replica")
    tokens, features = context.shape
    per_adapter, _, rank_extent = adapter_down.shape
    slots = tokens // 2 // CHUNKS
    wide = per_adapter * rank_extent
    tile = min(512, features)
    chips = tensors // CORES

    target = token_adapter // per_adapter
    within = token_adapter % per_adapter
    onehot = (target[:, None] == jnp.arange(owners)[None, :]).astype(BF16)
    before = (jnp.arange(tokens)[:, None] > jnp.arange(tokens)[None, :]).astype(BF16)
    counts = jnp.dot(before, onehot, preferred_element_type=F32)
    rank = jnp.sum(counts * onehot.astype(F32), axis=1).astype(jnp.int32)
    slot = (rank // slots * owners + target) * slots + rank % slots
    hit = slot[:, None] == jnp.arange(CHUNKS * owners * slots)[None, :]
    place = hit.astype(BF16)
    ids = jnp.max(jnp.where(hit, within[:, None], -1), axis=0).reshape(CHUNKS, owners, slots)
    ids = ids.transpose(1, 0, 2).reshape(owners, 1, CHUNKS * slots)
    ids = jnp.broadcast_to(ids, (owners, 8, CHUNKS * slots))
    place = place.reshape(tokens, CHUNKS, owners * slots).transpose(1, 0, 2)

    late = rank >= slots
    order = jnp.dot(before, late.astype(BF16)[:, None], preferred_element_type=F32)[:, 0]
    listed = late[:, None] & (order.astype(jnp.int32)[:, None] == jnp.arange(slots)[None, :])
    extra = listed.astype(BF16)
    overflow = (jnp.sum(late.astype(jnp.int32)) > slots).astype(jnp.int32)
    extra_ids = jnp.max(
        jnp.where(
            listed[None] & (target[None, :] == jnp.arange(owners)[:, None])[:, :, None],
            within[None, :, None],
            -1,
        ),
        axis=1,
    )
    fast_ids = jnp.concatenate([ids[:, 0, :slots], extra_ids], axis=1)[:, None, :]
    fast_ids = jnp.concatenate(
        [fast_ids, jnp.full((owners, 7, CHUNKS * slots), overflow, jnp.int32)], axis=1
    )

    anywhere = pl.BlockSpec(memory_space=pl.ANY)
    vmem = pl.BlockSpec(memory_space=pltpu.VMEM)
    dma = pltpu.SemaphoreType.DMA
    scratch = lambda depth: [
        pltpu.VMEM((depth, owners, slots, features), BF16),
        pltpu.VMEM((CHUNKS, owners, slots, features), BF16),
        pltpu.VMEM((owners, 8, CHUNKS * slots), jnp.int32),
        pltpu.VMEM((wide, features), BF16),
        pltpu.VMEM((wide, features), BF16),
        pltpu.VMEM((2, features, tile), BF16),
        pltpu.VMEM((chips - 1, tokens, features), BF16),
        pltpu.VMEM((chips - 1, tokens, features), BF16),
        pltpu.VMEM((chips - 1, tokens, features), BF16),
        pltpu.VMEM((chips - 1, tokens, features), BF16),
        pltpu.VMEM((tokens, features), BF16),
        pltpu.VMEM((tokens, features), BF16),
        pltpu.VMEM((tokens, features), F32),
        pltpu.VMEM((CHUNKS, owners * slots, 2 * rank_extent), BF16),
        pltpu.VMEM((CHUNKS, tensors - 1, owners * slots, 2 * rank_extent), BF16),
        pltpu.VMEM((CHUNKS, owners, slots, features), BF16),
        pltpu.VMEM((depth, owners, slots, features), BF16),
        dma((2,)),
        dma((3,)),
        dma((owners - 1,)),
        dma((owners - 1,)),
        dma((CHUNKS, owners - 1)),
        dma((CHUNKS, owners - 1)),
        dma((chips - 1,)),
        dma((chips - 1,)),
        dma((chips - 1,)),
        dma((chips - 1,)),
        dma,
        dma,
        dma((CHUNKS, tensors - 1)),
        dma((CHUNKS, tensors - 1)),
        dma((CHUNKS, owners - 1)),
        dma((CHUNKS, owners - 1)),
    ]
    projected, flag = pl.pallas_call(
        functools.partial(fast_kernel, owners, tensors, tile, rank_extent),
        out_shape=(
            jax.ShapeDtypeStruct((tokens, features), BF16),
            jax.ShapeDtypeStruct((8, CHUNKS * slots), jnp.int32),
        ),
        in_specs=[vmem, anywhere, anywhere, anywhere, anywhere, vmem, vmem],
        out_specs=(vmem, vmem),
        scratch_shapes=scratch(1)
        + [
            pltpu.VMEM((2, owners, slots, features), BF16),
            pltpu.VMEM((replicas, 8, CHUNKS * slots), jnp.int32),
            dma((2, owners)),
            dma((owners,)),
            dma((2, owners)),
            dma((2, owners)),
            dma((replicas - 1,)),
            dma((replicas - 1,)),
        ],
        compiler_params=pltpu.CompilerParams(
            collective_id=0, has_side_effects=True, vmem_limit_bytes=60 * 1024 * 1024
        ),
        cost_estimate=pl.CostEstimate(
            flops=2 * tokens * features * features * tensors,
            bytes_accessed=2 * features * features * tensors,
            transcendentals=0,
        ),
    )(
        context,
        output_weight,
        adapter_down.transpose(0, 2, 1).reshape(wide, features),
        adapter_up.reshape(wide, features),
        fast_ids,
        place[:1],
        extra,
    )

    def whole(ids, place):
      return pl.pallas_call(
        functools.partial(kernel, owners, tensors, tile, rank_extent),
        out_shape=jax.ShapeDtypeStruct((tokens, features), BF16),
        in_specs=[vmem, anywhere, anywhere, anywhere, anywhere, vmem],
        out_specs=vmem,
        scratch_shapes=scratch(CHUNKS),
        compiler_params=pltpu.CompilerParams(
            collective_id=1, has_side_effects=True, vmem_limit_bytes=60 * 1024 * 1024
        ),
        cost_estimate=pl.CostEstimate(
            flops=2 * tokens * features * features * tensors,
            bytes_accessed=2 * features * features * tensors,
            transcendentals=0,
        ),
    )(
        context,
        output_weight,
        adapter_down.transpose(0, 2, 1).reshape(wide, features),
        adapter_up.reshape(wide, features),
        ids,
        place,
    )

    return lax.cond(
        flag[1, 0] > 0, lambda: whole(ids, place), lambda: projected
    )


def solution(mesh):
    placed = (
        P(("replica", "owner"), "tensor"),
        P("tensor", None),
        P("owner", "tensor", None),
        P("owner", None, "tensor"),
        P(("replica", "owner")),
    )
    return jax.shard_map(
        on_device,
        mesh=mesh,
        in_specs=placed,
        out_specs=P(("replica", "owner"), "tensor"),
        check_vma=False,
    )
```
